512 devices in a mesh: kx: 4 (over z_lo), ky: 4 (over x), kz: 4 (over z_hi, core), fft: 8 (over y).
Axes of the slice: x: 4, y: 8, z: 8 (z_hi: 2, z_lo: 4; z = z_hi * 4 + z_lo), core: 2. Of those that a mesh axis runs over, the one named last changes fastest.
Arguments:
- occupied: bfloat16 [4, 4, 4, 2, 2, 96, 96, 128], P('kx', 'ky', 'kz', None, None, 'fft'), may hold values from -6 to 6
- targets: bfloat16 [4, 4, 4, 2, 2, 96, 96, 128], P('kx', 'ky', 'kz', None, None, 'fft'), may hold values from -6 to 6
- weights: bfloat16 [4, 4, 4, 2], P('kx', 'ky', 'kz'), may hold values from 0.19921875 to 2
- kernel: bfloat16 [96, 96, 128], P(None, 'fft'), may hold values from 0.099609375 to 4
Outputs:
- exchanged: bfloat16 [4, 4, 4, 2, 2, 96, 96, 128], P('kx', 'ky', 'kz', None, None, 'fft')
The draws below stay inside these ranges and needn't reach their ends.
All inputs are finite; a program needn't handle non-finite values.
Results may differ from the reference program's by a relative error of at most 0.0095.
Values may be sent and summed in bfloat16 or wider, within the bound.
A program may use at most 64 MiB of HBM per device.

```python
import math
import jax
import jax.numpy as jnp
from jax import lax

GRID_A = 96
GRID_B = 96
GRID_C = 128
OCC_BANDS = 2
TGT_BANDS = 2
KPT_X = 4
KPT_Y = 4
KPT_Z = 4


def steps_of(own_key, extent, shards, smallest, high):
    def one(dim, parts):
        steps = jax.random.uniform(jax.random.fold_in(jax.random.fold_in(own_key, 6), dim), (parts,), jnp.float32, smallest / len(shards), high / len(shards))
        return jnp.repeat(jnp.exp(steps), extent[dim] // parts).reshape((-1,) + (1,) * (len(extent) - dim - 1))

    factor_of = one(*shards[0])
    for cut in shards[1:]:
        factor_of = factor_of * one(*cut)
    return factor_of


def normal_values(key, shape, deviation, reach, split=(), kind=jnp.bfloat16):
    values = deviation * jax.random.normal(key, shape, jnp.float32)
    if split:
        values = values * steps_of(key, shape, split, -0.22, 0.18)
    return jnp.clip(values, -reach, reach).astype(kind)


def setup_inputs(seed: int = 0) -> dict:
    arg_keys = jax.random.split(jax.random.key(seed), 5)
    occupied = normal_values(arg_keys[0], (KPT_X, KPT_Y, KPT_Z, 2, OCC_BANDS, GRID_A, GRID_B, GRID_C), 1.0, 6.0, ((0, 4), (1, 4), (2, 4), (5, 8)))
    targets = normal_values(arg_keys[1], (KPT_X, KPT_Y, KPT_Z, 2, TGT_BANDS, GRID_A, GRID_B, GRID_C), 1.0, 6.0, ((0, 4), (1, 4), (2, 4), (5, 8)))
    weights = jnp.clip(0.19921875 + 1.8007812 * jax.random.uniform(arg_keys[2], (KPT_X, KPT_Y, KPT_Z, OCC_BANDS), jnp.float32) ** steps_of(arg_keys[2], (KPT_X, KPT_Y, KPT_Z, OCC_BANDS), ((0, 4), (1, 4), (2, 4)), -0.2, 0.2), 0.19921875, 2.0).astype(jnp.bfloat16)
    kernel = jnp.clip(jnp.exp(math.log(4.0) - 3.6927934 * jax.random.uniform(arg_keys[3], (GRID_A, GRID_B, GRID_C), jnp.float32) ** steps_of(arg_keys[3], (GRID_A, GRID_B, GRID_C), ((1, 8),), -0.2, 0.2)), 0.099609375, 4.0).astype(jnp.bfloat16)
    return {"occupied": occupied, "targets": targets, "weights": weights, "kernel": kernel}


def dft_table(length, sign):
    index = jnp.arange(length, dtype=jnp.int32)
    phase = index[:, None] * index[None, :] % length
    theta = phase.astype(jnp.float32) * (2.0 * math.pi / length)
    factor = 1.0 / math.sqrt(length)
    cosine = jnp.cos(theta) * factor
    sine = jnp.sin(theta) * (sign * factor)
    return jnp.stack([jnp.stack([cosine, -sine]), jnp.stack([sine, cosine])]).astype(jnp.bfloat16)

def transform(field, table, form):
    return jnp.einsum(form, table.astype(jnp.float32), field.astype(jnp.float32), precision=lax.Precision.HIGHEST)

def one_group(operands, kernel):
    occ, tgt, wts = operands
    occ_re = occ[0][:, None].astype(jnp.float32)
    occ_im = occ[1][:, None].astype(jnp.float32)
    tgt_re = tgt[0][None].astype(jnp.float32)
    tgt_im = tgt[1][None].astype(jnp.float32)
    pair = jnp.stack([occ_re * tgt_re + occ_im * tgt_im, occ_re * tgt_im - occ_im * tgt_re]).astype(jnp.bfloat16)
    pair = pair.reshape((2, OCC_BANDS * TGT_BANDS, GRID_A, GRID_B, GRID_C))
    first = transform(pair, dft_table(GRID_C, -1.0), 'oikj,ipabj->opabk').astype(jnp.bfloat16)
    second = transform(first, dft_table(GRID_B, -1.0), 'oikj,ipajc->opakc').astype(jnp.bfloat16)
    spectrum = transform(second, dft_table(GRID_A, -1.0), 'oikj,ipjbc->opkbc')
    screened = (spectrum * kernel.astype(jnp.float32)).astype(jnp.bfloat16)
    back_one = transform(screened, dft_table(GRID_A, 1.0), 'oikj,ipjbc->opkbc').astype(jnp.bfloat16)
    back_two = transform(back_one, dft_table(GRID_B, 1.0), 'oikj,ipajc->opakc').astype(jnp.bfloat16)
    potential = transform(back_two, dft_table(GRID_C, 1.0), 'oikj,ipabj->opabk')
    potential = potential.reshape((2, OCC_BANDS, TGT_BANDS, GRID_A, GRID_B, GRID_C))
    scaled = wts.astype(jnp.float32)[:, None, None, None, None]
    orb_re = occ[0].astype(jnp.float32)[:, None] * scaled
    orb_im = occ[1].astype(jnp.float32)[:, None] * scaled
    real_part = lax.optimization_barrier(jnp.sum(orb_re * potential[0] - orb_im * potential[1], axis=0))
    imag_part = lax.optimization_barrier(jnp.sum(orb_re * potential[1] + orb_im * potential[0], axis=0))
    return (-0.25 * jnp.stack([real_part, imag_part])).astype(jnp.bfloat16)

def reference(occupied, targets, weights, kernel):
    groups = KPT_X * KPT_Y * KPT_Z
    shifted = jnp.roll(occupied, (1, 1, 1), axis=(0, 1, 2))
    shifted_weights = jnp.roll(weights, (1, 1, 1), axis=(0, 1, 2))
    occ_all = shifted.reshape((groups, 2, OCC_BANDS, GRID_A, GRID_B, GRID_C))
    tgt_all = targets.reshape((groups, 2, TGT_BANDS, GRID_A, GRID_B, GRID_C))
    wts_all = shifted_weights.reshape((groups, OCC_BANDS))
    result = lax.map(lambda operands: one_group(operands, kernel), (occ_all, tgt_all, wts_all))
    return result.reshape((KPT_X, KPT_Y, KPT_Z, 2, TGT_BANDS, GRID_A, GRID_B, GRID_C))
```

```python
import functools
import math

import jax
import jax.numpy as jnp
import ml_dtypes
import numpy as np
from jax import lax
from jax.experimental import pallas as pl
from jax.experimental.pallas import tpu as pltpu
from jax.sharding import PartitionSpec as P

MESH = pl.DeviceIdType.MESH
CHUNK = 4
GROUP = 4
TILE = CHUNK * GROUP


def dft_table(length, sign):
    index = np.arange(length)
    theta = (index[:, None] * index[None, :] % length) * (2.0 * math.pi / length)
    factor = 1.0 / math.sqrt(length)
    cosine = np.cos(theta) * factor
    sine = np.sin(theta) * (sign * factor)
    return np.stack([np.stack([cosine, -sine]), np.stack([sine, cosine])])


def tables(ring, planes, width_b, width_c):
    width_a = ring * planes
    slab = width_b // ring
    chunks = planes // CHUNK

    def c_table(sign):
        table = dft_table(width_c, sign)
        return table.transpose(1, 3, 0, 2).reshape(2 * width_c, 2 * width_c)

    forward = dft_table(width_b, -1.0).reshape(2, 2, ring, slab, width_b)
    b_forward = forward.transpose(2, 0, 3, 1, 4).reshape(2 * width_b, 2 * width_b)
    inverse = dft_table(width_b, 1.0).reshape(2, 2, width_b, ring, slab)
    b_inverse = inverse.transpose(0, 2, 3, 1, 4).reshape(2 * width_b, 2 * width_b)

    same = np.eye(GROUP)
    forward = dft_table(width_a, -1.0).reshape(2, 2, width_a, ring, chunks, CHUNK)
    a_forward = np.einsum("oikyja,gh->ogkjyiha", forward, same)
    a_forward = a_forward.reshape(2 * GROUP * width_a, 2 * GROUP * width_a)
    inverse = dft_table(width_a, 1.0).reshape(2, 2, ring, chunks, CHUNK, width_a)
    a_inverse = np.einsum("oiyjak,gh->jyogaihk", inverse, same)
    a_inverse = a_inverse.reshape(2 * GROUP * width_a, 2 * GROUP * width_a)
    return [
        t.astype(ml_dtypes.bfloat16)
        for t in (c_table(-1.0), c_table(1.0), b_forward, b_inverse, a_forward, a_inverse)
    ]


def dot(x, y):
    return jnp.dot(x, y, preferred_element_type=jnp.float32)


def kernel_body(
    dims,
    occ_hbm, tgt_hbm, w_ref, ker_hbm, c1_hbm, c2_hbm, b1_hbm, b2_hbm, a1_hbm, a2_hbm,
    out_hbm,
    occ, tgt, ker, c1, c2, b1, b2, a1, a2, w_own, w_got,
    ker_rows, ker_t, mixed, send1, recv1, send2, recv2, acc, out,
    load_sem, shift_send, shift_recv, w_send, w_recv,
    send1_sem, recv1_sem, send2_sem, recv2_sem, out_sem,
):
    sizes, bands, targets, planes, width_b, width_c = dims
    ring = sizes["fft"]
    chunks = planes // CHUNK
    slab = width_b // ring
    groups = slab // GROUP
    width_a = ring * planes
    rows = CHUNK * width_b
    me = lax.axis_index("fft")

    def moved(by):
        return {
            axis: lax.rem(lax.axis_index(axis) + (sizes[axis] + by), sizes[axis])
            for axis in ("kx", "ky", "kz")
        }

    ahead, behind = moved(1), moved(-1)
    order = [d for pair in zip(range(ring // 2, 0, -1), range(ring // 2, ring)) for d in pair]
    order = list(dict.fromkeys(order))

    def partner(d):
        return lax.rem(me + d, ring)

    barrier = pltpu.get_barrier_semaphore()
    for device in (ahead, behind):
        pl.semaphore_signal(barrier, inc=1, device_id=device, device_id_type=MESH)
    for d in order:
        pl.semaphore_signal(barrier, inc=1, device_id={"fft": partner(d)}, device_id_type=MESH)

    loads = [
        pltpu.make_async_copy(src, dst, load_sem.at[i])
        for i, (src, dst) in enumerate(
            (
                (tgt_hbm, tgt), (c1_hbm, c1), (b1_hbm, b1), (ker_hbm, ker),
                (a1_hbm, a1), (a2_hbm, a2), (b2_hbm, b2), (c2_hbm, c2),
            )
        )
    ]
    for load in loads:
        load.start()
    for m in range(bands):
        w_own[m] = jnp.broadcast_to(
            w_ref[:, m : m + 1].astype(jnp.float32), w_own.shape[1:]
        ).astype(jnp.bfloat16)

    pl.semaphore_wait(barrier, 2 + ring - 1)

    def shift(m, j):
        part = (slice(None), m, pl.ds(j * CHUNK, CHUNK))
        return pltpu.make_async_remote_copy(
            src_ref=occ_hbm.at[part],
            dst_ref=occ.at[part],
            send_sem=shift_send.at[m, j],
            recv_sem=shift_recv.at[m, j],
            device_id=ahead,
            device_id_type=MESH,
        )

    w_copy = pltpu.make_async_remote_copy(
        src_ref=w_own, dst_ref=w_got, send_sem=w_send, recv_sem=w_recv,
        device_id=ahead, device_id_type=MESH,
    )
    for m in range(bands):
        for j in range(chunks):
            shift(m, j).start()
    w_copy.start()

    def scatter(p, j, send, recv, send_sem, recv_sem):
        for d in order:
            to = partner(d)
            pltpu.make_async_remote_copy(
                src_ref=send.at[p, j, to],
                dst_ref=recv.at[p, j, me],
                send_sem=send_sem.at[p, j],
                recv_sem=recv_sem.at[p, j],
                device_id={"fft": to},
                device_id_type=MESH,
            ).start()
        pltpu.make_async_copy(send.at[p, j, me], recv.at[p, j, me], recv_sem.at[p, j]).start()

    def gathered(p, j, recv, recv_sem):
        pltpu.make_async_copy(recv.at[p, j], recv.at[p, j], recv_sem.at[p, j]).wait()

    loads[3].wait()
    for k in range(width_a):
        ker_rows[pl.ds(k * 2 * 8, slab), :] = ker[k].astype(jnp.float32)
    for b in range(slab):
        ker_t[b // GROUP, pl.ds(b % GROUP * width_a, width_a), :] = ker_rows[
            pl.ds(b, width_a, stride=2 * 8), :
        ]

    for i in (0, 1, 2):
        loads[i].wait()

    def forward(step, _):
        m, j = step // chunks, lax.rem(step, chunks)
        shift(m, j).wait_recv()
        here = pl.ds(j * CHUNK, CHUNK)
        o_re = occ[0, m, here].reshape(rows, width_c).astype(jnp.float32)
        o_im = occ[1, m, here].reshape(rows, width_c).astype(jnp.float32)
        for n in range(targets):
            p = m * targets + n
            t_re = tgt[0, n, here].reshape(rows, width_c).astype(jnp.float32)
            t_im = tgt[1, n, here].reshape(rows, width_c).astype(jnp.float32)
            pair = jnp.concatenate(
                [
                    (o_re * t_re + o_im * t_im).astype(jnp.bfloat16),
                    (o_re * t_im - o_im * t_re).astype(jnp.bfloat16),
                ],
                axis=1,
            )
            first = dot(pair, c1[...]).astype(jnp.bfloat16)
            for a in range(0, CHUNK, 2):
                both = [first[k * width_b : (k + 1) * width_b] for k in (a, a + 1)]
                lines = jnp.concatenate(
                    [
                        jnp.concatenate([x[:, :width_c] for x in both], axis=1),
                        jnp.concatenate([x[:, width_c:] for x in both], axis=1),
                    ],
                    axis=0,
                )
                second = dot(b1[...], lines)
                mixed[pl.ds(a, 2 * width_b, stride=CHUNK), :] = second[:, :width_c]
                mixed[pl.ds(a + 1, 2 * width_b, stride=CHUNK), :] = second[:, width_c:]
            send1[p, j] = mixed[...].astype(jnp.bfloat16).reshape(send1.shape[2:])
            scatter(p, j, send1, recv1, send1_sem, recv1_sem)
        return 0

    lax.fori_loop(0, bands * chunks, forward, 0)

    for i in (4, 5, 6, 7):
        loads[i].wait()

    def middle(p, _):
        for j in range(chunks):
            gathered(p, j, recv1, recv1_sem)
        lines = jnp.concatenate(
            [
                recv1[p, :, :, :, g * TILE : (g + 1) * TILE, :].reshape(2 * GROUP * width_a, width_c)
                for g in range(groups)
            ],
            axis=1,
        )
        spectrum = dot(a1[...], lines)
        half = GROUP * width_a
        screened = jnp.concatenate(
            [
                jnp.concatenate(
                    [
                        spectrum[i * half : (i + 1) * half, g * width_c : (g + 1) * width_c] * ker_t[g]
                        for g in range(groups)
                    ],
                    axis=1,
                ).astype(jnp.bfloat16)
                for i in range(2)
            ],
            axis=0,
        )
        back = dot(a2[...], screened).astype(jnp.bfloat16)
        for g in range(groups):
            send2[p, :, :, :, g * TILE : (g + 1) * TILE, :] = back[
                :, g * width_c : (g + 1) * width_c
            ].reshape(chunks, ring, 2, TILE, width_c)
        for j in range(chunks):
            scatter(p, j, send2, recv2, send2_sem, recv2_sem)
        return 0

    lax.fori_loop(0, bands * targets, middle, 0)

    w_copy.wait_recv()

    def backward(m, step):
        n, j = step // chunks, lax.rem(step, chunks)
        p = m * targets + n
        gathered(p, j, recv2, recv2_sem)
        mixed[...] = recv2[p, j].reshape(mixed.shape).astype(jnp.float32)
        two = []
        for a in range(0, CHUNK, 2):
            lines = jnp.concatenate(
                [mixed[pl.ds(k, 2 * width_b, stride=CHUNK), :] for k in (a, a + 1)], axis=1
            ).astype(jnp.bfloat16)
            done = dot(b2[...], lines).astype(jnp.bfloat16)
            for k in range(2):
                cut = done[:, k * width_c : (k + 1) * width_c]
                two.append(jnp.concatenate([cut[:width_b], cut[width_b:]], axis=1))
        potential = dot(jnp.concatenate(two, axis=0), c2[...])
        v_re, v_im = potential[:, :width_c], potential[:, width_c:]
        here = pl.ds(j * CHUNK, CHUNK)
        scale = w_got[m].astype(jnp.float32)[:1]
        o_re = occ[0, m, here].reshape(rows, width_c).astype(jnp.float32) * scale
        o_im = occ[1, m, here].reshape(rows, width_c).astype(jnp.float32) * scale
        sums = (o_re * v_re - o_im * v_im, o_re * v_im + o_im * v_re)
        for i in range(2):
            if m > 0:
                total = acc[i, n, j] + sums[i]
            else:
                total = sums[i]
            if m == bands - 1:
                out[i, n, here] = (-0.25 * total).astype(jnp.bfloat16).reshape(
                    CHUNK, width_b, width_c
                )
            else:
                acc[i, n, j] = total
        if m == bands - 1:
            store(n, j).start()
        return 0

    def store(n, j):
        part = (slice(None), n, pl.ds(j * CHUNK, CHUNK))
        return pltpu.make_async_copy(out.at[part], out_hbm.at[part], out_sem.at[n, j])

    for m in range(bands):
        lax.fori_loop(0, targets * chunks, lambda step, _, m=m: backward(m, step), 0)

    w_copy.wait_send()

    def drain_shift(step, _):
        shift(step // chunks, lax.rem(step, chunks)).wait_send()
        return 0

    lax.fori_loop(0, bands * chunks, drain_shift, 0)

    def drain(step, _):
        p, j = step // chunks, lax.rem(step, chunks)
        for send, sem in ((send1, send1_sem), (send2, send2_sem)):
            gone = send.at[p, j, pl.ds(0, ring - 1)]
            pltpu.make_async_copy(gone, gone, sem.at[p, j]).wait()
        return 0

    lax.fori_loop(0, bands * targets * chunks, drain, 0)

    def drain_out(step, _):
        store(step // chunks, lax.rem(step, chunks)).wait()
        return 0

    lax.fori_loop(0, targets * chunks, drain_out, 0)


def shards(occupied, targets, weights, kernel, sizes):
    occ = occupied[0, 0, 0]
    tgt = targets[0, 0, 0]
    bands, tgts = occ.shape[1], tgt.shape[1]
    planes, width_b, width_c = occ.shape[2:]
    ring = sizes["fft"]
    width_a = ring * planes
    slab = width_b // ring
    chunks = planes // CHUNK
    groups = slab // GROUP
    pairs = bands * tgts
    constants = [jnp.asarray(t) for t in tables(ring, planes, width_b, width_c)]
    bf16, f32 = jnp.bfloat16, jnp.float32
    blocks = (pairs, chunks, ring, 2, slab * CHUNK, width_c)
    any_space = pl.BlockSpec(memory_space=pl.ANY)
    result = pl.pallas_call(
        functools.partial(kernel_body, (sizes, bands, tgts, planes, width_b, width_c)),
        out_shape=jax.ShapeDtypeStruct(tgt.shape, bf16),
        in_specs=[any_space, any_space, pl.BlockSpec(memory_space=pltpu.VMEM)] + [any_space] * 7,
        out_specs=any_space,
        scratch_shapes=[
            pltpu.VMEM(occ.shape, bf16),
            pltpu.VMEM(tgt.shape, bf16),
            pltpu.VMEM(kernel.shape, bf16),
            *[pltpu.VMEM(t.shape, bf16) for t in constants],
            pltpu.VMEM((bands, 16, width_c), bf16),
            pltpu.VMEM((bands, 16, width_c), bf16),
            pltpu.VMEM((width_a * 16, width_c), f32),
            pltpu.VMEM((groups, GROUP * width_a, width_c), f32),
            pltpu.VMEM((2 * width_b * CHUNK, width_c), f32),
            *[pltpu.VMEM(blocks, bf16)] * 4,
            pltpu.VMEM((2, tgts, chunks, CHUNK * width_b, width_c), f32),
            pltpu.VMEM(tgt.shape, bf16),
            pltpu.SemaphoreType.DMA((8,)),
            pltpu.SemaphoreType.DMA((bands, chunks)),
            pltpu.SemaphoreType.DMA((bands, chunks)),
            pltpu.SemaphoreType.DMA,
            pltpu.SemaphoreType.DMA,
            *[pltpu.SemaphoreType.DMA((pairs, chunks))] * 4,
            pltpu.SemaphoreType.DMA((tgts, chunks)),
        ],
        compiler_params=pltpu.CompilerParams(
            collective_id=0, has_side_effects=True, vmem_limit_bytes=56 << 20
        ),
    )(occ, tgt, weights.reshape(1, bands), kernel, *constants)
    return result[None, None, None]


def solution(mesh):
    return jax.shard_map(
        functools.partial(shards, sizes=dict(mesh.shape)),
        mesh=mesh,
        in_specs=(
            P("kx", "ky", "kz", None, None, "fft", None, None),
            P("kx", "ky", "kz", None, None, "fft", None, None),
            P("kx", "ky", "kz", None),
            P(None, "fft", None),
        ),
        out_specs=P("kx", "ky", "kz", None, None, "fft", None, None),
        check_vma=False,
    )
```

```python
import functools
import math

import jax
import jax.numpy as jnp
import ml_dtypes
import numpy as np
from jax import lax
from jax.experimental import pallas as pl
from jax.experimental.pallas import tpu as pltpu
from jax.sharding import PartitionSpec as P

MESH = pl.DeviceIdType.MESH
CHUNK = 2
GROUP = 4
TILE = GROUP * 2 * CHUNK


def dft_table(length, sign):
    index = np.arange(length)
    theta = (index[:, None] * index[None, :] % length) * (2.0 * math.pi / length)
    factor = 1.0 / math.sqrt(length)
    cosine = np.cos(theta) * factor
    sine = np.sin(theta) * (sign * factor)
    return np.stack([np.stack([cosine, -sine]), np.stack([sine, cosine])])


def tables(ring, planes, width_b, width_c):
    width_a = ring * planes
    slab = width_b // ring
    chunks = planes // CHUNK

    def c_table(sign):
        table = dft_table(width_c, sign)
        return table.transpose(1, 3, 0, 2).reshape(2 * width_c, 2 * width_c)

    forward = dft_table(width_b, -1.0).reshape(2, 2, ring, slab, width_b)
    b_forward = forward.transpose(2, 3, 0, 1, 4).reshape(2 * width_b, 2 * width_b)
    inverse = dft_table(width_b, 1.0).reshape(2, 2, width_b, ring, slab)
    b_inverse = inverse.transpose(0, 2, 3, 4, 1).reshape(2 * width_b, 2 * width_b)

    same = np.eye(GROUP)
    forward = dft_table(width_a, -1.0).reshape(2, 2, width_a, ring, chunks, CHUNK)
    a_forward = np.einsum("oikyja,gh->ogkjyhia", forward, same)
    a_forward = a_forward.reshape(2 * GROUP * width_a, 2 * GROUP * width_a)
    inverse = dft_table(width_a, 1.0).reshape(2, 2, ring, chunks, CHUNK, width_a)
    a_inverse = np.einsum("oiyjak,gh->jygoaihk", inverse, same)
    a_inverse = a_inverse.reshape(2 * GROUP * width_a, 2 * GROUP * width_a)
    return [
        t.astype(ml_dtypes.bfloat16)
        for t in (c_table(-1.0), c_table(1.0), b_forward, b_inverse, a_forward, a_inverse)
    ]


def dot(x, y):
    return jnp.dot(x, y, preferred_element_type=jnp.float32)


def kernel_body(
    dims,
    occ_hbm, tgt_hbm, w_ref, ker_hbm, c1_hbm, c2_hbm, b1_hbm, b2_hbm, a1_hbm, a2_hbm,
    out_hbm,
    occ, tgt, ker, c1, c2, b1, b2, a1, a2, w_own, w_got,
    mixed, send1, recv1, send2, recv2, acc, out,
    ready, load_sem, shift_send, shift_recv, w_send, w_recv,
    send1_sem, recv1_sem, send2_sem, recv2_sem, out_sem,
):
    sizes, bands, targets, planes, width_b, width_c = dims
    ring = sizes["fft"]
    chunks = planes // CHUNK
    slab = width_b // ring
    groups = slab // GROUP
    width_a = ring * planes
    rows = CHUNK * width_b
    me = lax.axis_index("fft")

    def moved(by):
        return {
            axis: lax.rem(lax.axis_index(axis) + (sizes[axis] + by), sizes[axis])
            for axis in ("kx", "ky", "kz")
        }

    ahead, behind = moved(1), moved(-1)
    order = [d for pair in zip(range(ring // 2, 0, -1), range(ring // 2, ring)) for d in pair]
    order = list(dict.fromkeys(order))

    def partner(d):
        return lax.rem(me + d, ring)

    place = lax.axis_index("kz")
    asks = place == sizes["kz"] // 2
    asked = place == sizes["kz"] // 2 - 1
    barrier = pltpu.get_barrier_semaphore()
    for d in order:
        pl.semaphore_signal(barrier, inc=1, device_id={"fft": partner(d)}, device_id_type=MESH)

    @pl.when(jnp.logical_not(asks))
    def _():
        pl.semaphore_signal(barrier, inc=1, device_id=behind, device_id_type=MESH)

    @pl.when(asked)
    def _():
        pl.semaphore_signal(barrier, inc=1, device_id=ahead, device_id_type=MESH)

    loads = [
        pltpu.make_async_copy(src, dst, load_sem.at[i])
        for i, (src, dst) in enumerate(
            (
                (tgt_hbm, tgt), (c1_hbm, c1), (b1_hbm, b1), (ker_hbm, ker),
                (a1_hbm, a1), (a2_hbm, a2), (b2_hbm, b2), (c2_hbm, c2),
            )
        )
    ]
    for load in loads:
        load.start()
    for m in range(bands):
        w_own[m] = jnp.broadcast_to(
            w_ref[:, m : m + 1].astype(jnp.float32), w_own.shape[1:]
        ).astype(jnp.bfloat16)

    pl.semaphore_wait(barrier, ring - 1 + jnp.where(asked, 0, 1) + jnp.where(asks, 1, 0))

    @pl.when(asks)
    def _():
        pl.semaphore_signal(ready, inc=1, device_id=behind, device_id_type=MESH)

    @pl.when(asked)
    def _():
        pl.semaphore_wait(ready, 1)

    def shift(m, j):
        part = (slice(None), m, pl.ds(j * CHUNK, CHUNK))
        return pltpu.make_async_remote_copy(
            src_ref=occ_hbm.at[part],
            dst_ref=occ.at[part],
            send_sem=shift_send.at[m, j],
            recv_sem=shift_recv.at[m, j],
            device_id=ahead,
            device_id_type=MESH,
        )

    w_copy = pltpu.make_async_remote_copy(
        src_ref=w_own, dst_ref=w_got, send_sem=w_send, recv_sem=w_recv,
        device_id=ahead, device_id_type=MESH,
    )
    for m in range(bands):
        for j in range(chunks):
            shift(m, j).start()
    w_copy.start()

    def scatter(p, j, send, recv, send_sem, recv_sem):
        for d in order:
            to = partner(d)
            pltpu.make_async_remote_copy(
                src_ref=send.at[p, j, to],
                dst_ref=recv.at[p, j, me],
                send_sem=send_sem.at[p, j],
                recv_sem=recv_sem.at[p, j],
                device_id={"fft": to},
                device_id_type=MESH,
            ).start()
        pltpu.make_async_copy(send.at[p, j, me], recv.at[p, j, me], recv_sem.at[p, j]).start()

    def gathered(p, j, recv, recv_sem):
        pltpu.make_async_copy(recv.at[p, j], recv.at[p, j], recv_sem.at[p, j]).wait()

    for i in (0, 1, 2):
        loads[i].wait()

    def forward(m, wanted, j):
        if 0 in wanted:
            shift(m, j).wait_recv()
        here = pl.ds(j * CHUNK, CHUNK)
        o_re = occ[0, m, here].reshape(rows, width_c).astype(jnp.float32)
        o_im = occ[1, m, here].reshape(rows, width_c).astype(jnp.float32)
        for n in wanted:
            p = m * targets + n
            t_re = tgt[0, n, here].reshape(rows, width_c).astype(jnp.float32)
            t_im = tgt[1, n, here].reshape(rows, width_c).astype(jnp.float32)
            pair = jnp.concatenate(
                [
                    (o_re * t_re + o_im * t_im).astype(jnp.bfloat16),
                    (o_re * t_im - o_im * t_re).astype(jnp.bfloat16),
                ],
                axis=1,
            )
            first = dot(pair, c1[...]).astype(jnp.bfloat16)
            for a in range(0, CHUNK, 2):
                both = [first[k * width_b : (k + 1) * width_b] for k in (a, a + 1)]
                lines = jnp.concatenate(
                    [
                        jnp.concatenate([x[:, :width_c] for x in both], axis=1),
                        jnp.concatenate([x[:, width_c:] for x in both], axis=1),
                    ],
                    axis=0,
                )
                second = dot(b1[...], lines)
                mixed[pl.ds(a, 2 * width_b, stride=CHUNK), :] = second[:, :width_c]
                mixed[pl.ds(a + 1, 2 * width_b, stride=CHUNK), :] = second[:, width_c:]
            send1[p, j] = mixed[...].astype(jnp.bfloat16).reshape(send1.shape[2:])
            scatter(p, j, send1, recv1, send1_sem, recv1_sem)
        return 0

    everything = tuple(range(targets))
    for m in range(bands):
        for wanted in (everything,) if m == 0 else tuple((n,) for n in everything):
            lax.fori_loop(0, chunks, lambda j, _, m=m, wanted=wanted: forward(m, wanted, j), 0)

    for i in (3, 4, 5, 6, 7):
        loads[i].wait()

    def middle(p, _):
        for j in range(chunks):
            gathered(p, j, recv1, recv1_sem)
        lines = jnp.concatenate(
            [
                recv1[p, :, :, g * TILE : (g + 1) * TILE, :].reshape(2 * GROUP * width_a, width_c)
                for g in range(groups)
            ],
            axis=1,
        )
        spectrum = dot(a1[...], lines)
        half = GROUP * width_a
        factor = [
            ker[g * GROUP : (g + 1) * GROUP].reshape(half, width_c).astype(jnp.float32)
            for g in range(groups)
        ]
        screened = jnp.concatenate(
            [
                jnp.concatenate(
                    [
                        spectrum[i * half : (i + 1) * half, g * width_c : (g + 1) * width_c] * factor[g]
                        for g in range(groups)
                    ],
                    axis=1,
                ).astype(jnp.bfloat16)
                for i in range(2)
            ],
            axis=0,
        )
        back = dot(a2[...], screened).astype(jnp.bfloat16)
        for g in range(groups):
            send2[p, :, :, g * TILE : (g + 1) * TILE, :] = back[
                :, g * width_c : (g + 1) * width_c
            ].reshape(chunks, ring, TILE, width_c)
        for j in range(chunks):
            scatter(p, j, send2, recv2, send2_sem, recv2_sem)
        return 0

    lax.fori_loop(0, bands * targets, middle, 0)

    w_copy.wait_recv()

    def backward(m, step):
        n, j = step // chunks, lax.rem(step, chunks)
        p = m * targets + n
        gathered(p, j, recv2, recv2_sem)
        mixed[...] = recv2[p, j].reshape(mixed.shape).astype(jnp.float32)
        two = []
        for a in range(0, CHUNK, 2):
            lines = jnp.concatenate(
                [mixed[pl.ds(k, 2 * width_b, stride=CHUNK), :] for k in (a, a + 1)], axis=1
            ).astype(jnp.bfloat16)
            done = dot(b2[...], lines).astype(jnp.bfloat16)
            for k in range(2):
                cut = done[:, k * width_c : (k + 1) * width_c]
                two.append(jnp.concatenate([cut[:width_b], cut[width_b:]], axis=1))
        potential = dot(jnp.concatenate(two, axis=0), c2[...])
        v_re, v_im = potential[:, :width_c], potential[:, width_c:]
        here = pl.ds(j * CHUNK, CHUNK)
        scale = w_got[m].astype(jnp.float32)[:1]
        o_re = occ[0, m, here].reshape(rows, width_c).astype(jnp.float32) * scale
        o_im = occ[1, m, here].reshape(rows, width_c).astype(jnp.float32) * scale
        sums = (o_re * v_re - o_im * v_im, o_re * v_im + o_im * v_re)
        for i in range(2):
            if m > 0:
                total = acc[i, n, j] + sums[i]
            else:
                total = sums[i]
            if m == bands - 1:
                out[i, n, here] = (-0.25 * total).astype(jnp.bfloat16).reshape(
                    CHUNK, width_b, width_c
                )
            else:
                acc[i, n, j] = total
        if m == bands - 1:
            store(n, j).start()
        return 0

    def store(n, j):
        part = (slice(None), n, pl.ds(j * CHUNK, CHUNK))
        return pltpu.make_async_copy(out.at[part], out_hbm.at[part], out_sem.at[n, j])

    for m in range(bands):
        lax.fori_loop(0, targets * chunks, lambda step, _, m=m: backward(m, step), 0)

    w_copy.wait_send()

    def drain_shift(step, _):
        shift(step // chunks, lax.rem(step, chunks)).wait_send()
        return 0

    lax.fori_loop(0, bands * chunks, drain_shift, 0)

    def drain(step, _):
        p, j = step // chunks, lax.rem(step, chunks)
        for send, sem in ((send1, send1_sem), (send2, send2_sem)):
            gone = send.at[p, j, pl.ds(0, ring - 1)]
            pltpu.make_async_copy(gone, gone, sem.at[p, j]).wait()
        return 0

    lax.fori_loop(0, bands * targets * chunks, drain, 0)

    def drain_out(step, _):
        store(step // chunks, lax.rem(step, chunks)).wait()
        return 0

    lax.fori_loop(0, targets * chunks, drain_out, 0)


def shards(occupied, targets, weights, kernel, sizes):
    occ = occupied[0, 0, 0]
    tgt = targets[0, 0, 0]
    bands, tgts = occ.shape[1], tgt.shape[1]
    planes, width_b, width_c = occ.shape[2:]
    ring = sizes["fft"]
    width_a = ring * planes
    slab = width_b // ring
    chunks = planes // CHUNK
    groups = slab // GROUP
    pairs = bands * tgts
    constants = [jnp.asarray(t) for t in tables(ring, planes, width_b, width_c)]
    bf16, f32 = jnp.bfloat16, jnp.float32
    blocks = (pairs, chunks, ring, slab * 2 * CHUNK, width_c)
    any_space = pl.BlockSpec(memory_space=pl.ANY)
    result = pl.pallas_call(
        functools.partial(kernel_body, (sizes, bands, tgts, planes, width_b, width_c)),
        out_shape=jax.ShapeDtypeStruct(tgt.shape, bf16),
        in_specs=[any_space, any_space, pl.BlockSpec(memory_space=pltpu.VMEM)] + [any_space] * 7,
        out_specs=any_space,
        scratch_shapes=[
            pltpu.VMEM(occ.shape, bf16),
            pltpu.VMEM(tgt.shape, bf16),
            pltpu.VMEM((slab, width_a, width_c), bf16),
            *[pltpu.VMEM(t.shape, bf16) for t in constants],
            pltpu.VMEM((bands, 16, width_c), bf16),
            pltpu.VMEM((bands, 16, width_c), bf16),
            pltpu.VMEM((2 * width_b * CHUNK, width_c), f32),
            *[pltpu.VMEM(blocks, bf16)] * 4,
            pltpu.VMEM((2, tgts, chunks, CHUNK * width_b, width_c), f32),
            pltpu.VMEM(tgt.shape, bf16),
            pltpu.SemaphoreType.REGULAR,
            pltpu.SemaphoreType.DMA((8,)),
            pltpu.SemaphoreType.DMA((bands, chunks)),
            pltpu.SemaphoreType.DMA((bands, chunks)),
            pltpu.SemaphoreType.DMA,
            pltpu.SemaphoreType.DMA,
            *[pltpu.SemaphoreType.DMA((pairs, chunks))] * 4,
            pltpu.SemaphoreType.DMA((tgts, chunks)),
        ],
        compiler_params=pltpu.CompilerParams(
            collective_id=0, has_side_effects=True, vmem_limit_bytes=56 << 20
        ),
    )(occ, tgt, weights.reshape(1, bands), kernel.transpose(1, 0, 2), *constants)
    return result[None, None, None]


def solution(mesh):
    return jax.shard_map(
        functools.partial(shards, sizes=dict(mesh.shape)),
        mesh=mesh,
        in_specs=(
            P("kx", "ky", "kz", None, None, "fft", None, None),
            P("kx", "ky", "kz", None, None, "fft", None, None),
            P("kx", "ky", "kz", None),
            P(None, "fft", None),
        ),
        out_specs=P("kx", "ky", "kz", None, None, "fft", None, None),
        check_vma=False,
    )
```

```python
import functools
import math

import jax
import jax.numpy as jnp
import ml_dtypes
import numpy as np
from jax import lax
from jax.experimental import pallas as pl
from jax.experimental.pallas import tpu as pltpu
from jax.sharding import PartitionSpec as P

MESH = pl.DeviceIdType.MESH
CHUNK = 2
GROUP = 4
TILE = GROUP * 2 * CHUNK


def dft_table(length, sign):
    index = np.arange(length)
    theta = (index[:, None] * index[None, :] % length) * (2.0 * math.pi / length)
    factor = 1.0 / math.sqrt(length)
    cosine = np.cos(theta) * factor
    sine = np.sin(theta) * (sign * factor)
    return np.stack([np.stack([cosine, -sine]), np.stack([sine, cosine])])


def tables(ring, planes, width_b, width_c):
    width_a = ring * planes
    slab = width_b // ring
    chunks = planes // CHUNK

    def c_table(sign):
        table = dft_table(width_c, sign)
        return table.transpose(1, 3, 0, 2).reshape(2 * width_c, 2 * width_c)

    forward = dft_table(width_b, -1.0).reshape(2, 2, ring, slab, width_b)
    b_forward = forward.transpose(2, 3, 0, 1, 4).reshape(2 * width_b, 2 * width_b)
    inverse = dft_table(width_b, 1.0).reshape(2, 2, width_b, ring, slab)
    b_inverse = inverse.transpose(0, 2, 3, 4, 1).reshape(2 * width_b, 2 * width_b)

    same = np.eye(GROUP)
    forward = dft_table(width_a, -1.0).reshape(2, 2, width_a, ring, chunks, CHUNK)
    a_forward = np.einsum("oikyja,gh->ogkjyhia", forward, same)
    a_forward = a_forward.reshape(2 * GROUP * width_a, 2 * GROUP * width_a)
    inverse = dft_table(width_a, 1.0).reshape(2, 2, ring, chunks, CHUNK, width_a)
    a_inverse = np.einsum("oiyjak,gh->jygoaihk", inverse, same)
    a_inverse = a_inverse.reshape(2 * GROUP * width_a, 2 * GROUP * width_a)
    return [
        t.astype(ml_dtypes.bfloat16)
        for t in (c_table(-1.0), c_table(1.0), b_forward, b_inverse, a_forward, a_inverse)
    ]


def dot(x, y):
    return jnp.dot(x, y, preferred_element_type=jnp.float32)


def kernel_body(
    dims,
    occ_hbm, tgt_hbm, w_ref, ker_hbm, c1_hbm, c2_hbm, b1_hbm, b2_hbm, a1_hbm, a2_hbm,
    out_hbm,
    occ, own, tgt, ker, c1, c2, b1, b2, a1, a2, w_own, w_got,
    mixed, send1, recv1, send2, recv2, acc, out,
    ready, load_sem, shift_send, shift_recv, w_send, w_recv,
    send1_sem, recv1_sem, send2_sem, recv2_sem, out_sem,
):
    sizes, bands, targets, planes, width_b, width_c = dims
    ring = sizes["fft"]
    chunks = planes // CHUNK
    slab = width_b // ring
    groups = slab // GROUP
    width_a = ring * planes
    rows = CHUNK * width_b
    me = lax.axis_index("fft")

    def moved(by):
        return {
            axis: lax.rem(lax.axis_index(axis) + (sizes[axis] + by), sizes[axis])
            for axis in ("kx", "ky", "kz")
        }

    ahead, behind = moved(1), moved(-1)
    order = [d for pair in zip(range(ring // 2, 0, -1), range(ring // 2, ring)) for d in pair]
    order = list(dict.fromkeys(order))

    def partner(d):
        return lax.rem(me + d, ring)

    place = lax.axis_index("kz")
    asks = place == sizes["kz"] // 2
    asked = place == sizes["kz"] // 2 - 1
    barrier = pltpu.get_barrier_semaphore()
    for d in order:
        pl.semaphore_signal(barrier, inc=1, device_id={"fft": partner(d)}, device_id_type=MESH)

    @pl.when(jnp.logical_not(asks))
    def _():
        pl.semaphore_signal(barrier, inc=1, device_id=behind, device_id_type=MESH)

    @pl.when(asked)
    def _():
        pl.semaphore_signal(barrier, inc=1, device_id=ahead, device_id_type=MESH)

    loads = [
        pltpu.make_async_copy(src, dst, load_sem.at[i])
        for i, (src, dst) in enumerate(
            (
                (tgt_hbm, tgt), (c1_hbm, c1), (b1_hbm, b1), (ker_hbm, ker),
                (a1_hbm, a1), (a2_hbm, a2), (b2_hbm, b2), (c2_hbm, c2), (occ_hbm, own),
            )
        )
    ]
    for load in loads[-1:] + loads[:-1]:
        load.start()
    for m in range(bands):
        w_own[m] = jnp.broadcast_to(
            w_ref[:, m : m + 1].astype(jnp.float32), w_own.shape[1:]
        ).astype(jnp.bfloat16)

    loads[-1].wait()
    pl.semaphore_wait(barrier, ring - 1 + jnp.where(asked, 0, 1) + jnp.where(asks, 1, 0))

    @pl.when(asks)
    def _():
        pl.semaphore_signal(ready, inc=1, device_id=behind, device_id_type=MESH)

    @pl.when(asked)
    def _():
        pl.semaphore_wait(ready, 1)

    def shift(m, j):
        part = (slice(None), m, pl.ds(j * CHUNK, CHUNK))
        return pltpu.make_async_remote_copy(
            src_ref=own.at[part],
            dst_ref=occ.at[part],
            send_sem=shift_send,
            recv_sem=shift_recv.at[m, j],
            device_id=ahead,
            device_id_type=MESH,
        )

    w_copy = pltpu.make_async_remote_copy(
        src_ref=w_own, dst_ref=w_got, send_sem=w_send, recv_sem=w_recv,
        device_id=ahead, device_id_type=MESH,
    )
    for m in range(bands):
        for j in range(chunks):
            shift(m, j).start()
    w_copy.start()

    def scatter(p, j, send, recv, send_sem, recv_sem):
        for d in order:
            to = partner(d)
            pltpu.make_async_remote_copy(
                src_ref=send.at[p, j, to],
                dst_ref=recv.at[p, j, me],
                send_sem=send_sem,
                recv_sem=recv_sem,
                device_id={"fft": to},
                device_id_type=MESH,
            ).start()
        pltpu.make_async_copy(send.at[p, j, me], recv.at[p, j, me], recv_sem).start()

    def ended(part, sem):
        pltpu.make_async_copy(part, part, sem).wait()

    for i in (0, 1, 2):
        loads[i].wait()

    def forward(step, _):
        m, j = step // chunks, lax.rem(step, chunks)
        shift(m, j).wait_recv()
        here = pl.ds(j * CHUNK, CHUNK)
        o_re = occ[0, m, here].reshape(rows, width_c).astype(jnp.float32)
        o_im = occ[1, m, here].reshape(rows, width_c).astype(jnp.float32)
        for n in range(targets):
            p = m * targets + n
            t_re = tgt[0, n, here].reshape(rows, width_c).astype(jnp.float32)
            t_im = tgt[1, n, here].reshape(rows, width_c).astype(jnp.float32)
            pair = jnp.concatenate(
                [
                    (o_re * t_re + o_im * t_im).astype(jnp.bfloat16),
                    (o_re * t_im - o_im * t_re).astype(jnp.bfloat16),
                ],
                axis=1,
            )
            first = dot(pair, c1[...]).astype(jnp.bfloat16)
            for a in range(0, CHUNK, 2):
                both = [first[k * width_b : (k + 1) * width_b] for k in (a, a + 1)]
                lines = jnp.concatenate(
                    [
                        jnp.concatenate([x[:, :width_c] for x in both], axis=1),
                        jnp.concatenate([x[:, width_c:] for x in both], axis=1),
                    ],
                    axis=0,
                )
                second = dot(b1[...], lines)
                mixed[pl.ds(a, 2 * width_b, stride=CHUNK), :] = second[:, :width_c]
                mixed[pl.ds(a + 1, 2 * width_b, stride=CHUNK), :] = second[:, width_c:]
            send1[p, j] = mixed[...].astype(jnp.bfloat16).reshape(send1.shape[2:])
            scatter(p, j, send1, recv1, send1_sem, recv1_sem.at[p])
        return 0

    lax.fori_loop(0, bands * chunks, forward, 0)

    for i in (3, 4, 5, 6, 7):
        loads[i].wait()

    def middle(p, _):
        ended(recv1.at[p], recv1_sem.at[p])
        lines = jnp.concatenate(
            [
                recv1[p, :, :, g * TILE : (g + 1) * TILE, :].reshape(2 * GROUP * width_a, width_c)
                for g in range(groups)
            ],
            axis=1,
        )
        spectrum = dot(a1[...], lines)
        half = GROUP * width_a
        factor = [
            ker[g * GROUP : (g + 1) * GROUP].reshape(half, width_c).astype(jnp.float32)
            for g in range(groups)
        ]
        screened = jnp.concatenate(
            [
                jnp.concatenate(
                    [
                        spectrum[i * half : (i + 1) * half, g * width_c : (g + 1) * width_c] * factor[g]
                        for g in range(groups)
                    ],
                    axis=1,
                ).astype(jnp.bfloat16)
                for i in range(2)
            ],
            axis=0,
        )
        back = dot(a2[...], screened).astype(jnp.bfloat16)
        for g in range(groups):
            send2[p, :, :, g * TILE : (g + 1) * TILE, :] = back[
                :, g * width_c : (g + 1) * width_c
            ].reshape(chunks, ring, TILE, width_c)
        for j in range(chunks):
            scatter(p, j, send2, recv2, send2_sem, recv2_sem.at[p, j])
        return 0

    lax.fori_loop(0, bands * targets, middle, 0)

    w_copy.wait()
    ended(occ, shift_send)
    ended(send1.at[:, :, pl.ds(0, ring - 1)], send1_sem)

    def backward(m, step):
        n, j = step // chunks, lax.rem(step, chunks)
        p = m * targets + n
        ended(recv2.at[p, j], recv2_sem.at[p, j])
        mixed[...] = recv2[p, j].reshape(mixed.shape).astype(jnp.float32)
        two = []
        for a in range(0, CHUNK, 2):
            lines = jnp.concatenate(
                [mixed[pl.ds(k, 2 * width_b, stride=CHUNK), :] for k in (a, a + 1)], axis=1
            ).astype(jnp.bfloat16)
            done = dot(b2[...], lines).astype(jnp.bfloat16)
            for k in range(2):
                cut = done[:, k * width_c : (k + 1) * width_c]
                two.append(jnp.concatenate([cut[:width_b], cut[width_b:]], axis=1))
        potential = dot(jnp.concatenate(two, axis=0), c2[...])
        v_re, v_im = potential[:, :width_c], potential[:, width_c:]
        here = pl.ds(j * CHUNK, CHUNK)
        scale = w_got[m].astype(jnp.float32)[:1]
        o_re = occ[0, m, here].reshape(rows, width_c).astype(jnp.float32) * scale
        o_im = occ[1, m, here].reshape(rows, width_c).astype(jnp.float32) * scale
        sums = (o_re * v_re - o_im * v_im, o_re * v_im + o_im * v_re)
        for i in range(2):
            if m > 0:
                total = acc[i, n, j] + sums[i]
            else:
                total = sums[i]
            if m == bands - 1:
                out[i, n, here] = (-0.25 * total).astype(jnp.bfloat16).reshape(
                    CHUNK, width_b, width_c
                )
            else:
                acc[i, n, j] = total
        if m == bands - 1:
            store(n, j).start()
        return 0

    def store(n, j):
        part = (slice(None), n, pl.ds(j * CHUNK, CHUNK))
        return pltpu.make_async_copy(out.at[part], out_hbm.at[part], out_sem)

    for m in range(bands):
        lax.fori_loop(0, targets * chunks, lambda step, _, m=m: backward(m, step), 0)

    ended(send2.at[:, :, pl.ds(0, ring - 1)], send2_sem)
    ended(out, out_sem)


def shards(occupied, targets, weights, kernel, sizes):
    occ = occupied[0, 0, 0]
    tgt = targets[0, 0, 0]
    bands, tgts = occ.shape[1], tgt.shape[1]
    planes, width_b, width_c = occ.shape[2:]
    ring = sizes["fft"]
    width_a = ring * planes
    slab = width_b // ring
    chunks = planes // CHUNK
    groups = slab // GROUP
    pairs = bands * tgts
    constants = [jnp.asarray(t) for t in tables(ring, planes, width_b, width_c)]
    bf16, f32 = jnp.bfloat16, jnp.float32
    blocks = (pairs, chunks, ring, slab * 2 * CHUNK, width_c)
    any_space = pl.BlockSpec(memory_space=pl.ANY)
    result = pl.pallas_call(
        functools.partial(kernel_body, (sizes, bands, tgts, planes, width_b, width_c)),
        out_shape=jax.ShapeDtypeStruct(tgt.shape, bf16),
        in_specs=[any_space, any_space, pl.BlockSpec(memory_space=pltpu.VMEM)] + [any_space] * 7,
        out_specs=any_space,
        scratch_shapes=[
            pltpu.VMEM(occ.shape, bf16),
            pltpu.VMEM(occ.shape, bf16),
            pltpu.VMEM(tgt.shape, bf16),
            pltpu.VMEM((slab, width_a, width_c), bf16),
            *[pltpu.VMEM(t.shape, bf16) for t in constants],
            pltpu.VMEM((bands, 16, width_c), bf16),
            pltpu.VMEM((bands, 16, width_c), bf16),
            pltpu.VMEM((2 * width_b * CHUNK, width_c), f32),
            *[pltpu.VMEM(blocks, bf16)] * 4,
            pltpu.VMEM((2, tgts, chunks, CHUNK * width_b, width_c), f32),
            pltpu.VMEM(tgt.shape, bf16),
            pltpu.SemaphoreType.REGULAR,
            pltpu.SemaphoreType.DMA((9,)),
            pltpu.SemaphoreType.DMA,
            pltpu.SemaphoreType.DMA((bands, chunks)),
            pltpu.SemaphoreType.DMA,
            pltpu.SemaphoreType.DMA,
            pltpu.SemaphoreType.DMA,
            pltpu.SemaphoreType.DMA((pairs,)),
            pltpu.SemaphoreType.DMA,
            pltpu.SemaphoreType.DMA((pairs, chunks)),
            pltpu.SemaphoreType.DMA,
        ],
        compiler_params=pltpu.CompilerParams(
            collective_id=0, has_side_effects=True, vmem_limit_bytes=56 << 20
        ),
    )(occ, tgt, weights.reshape(1, bands), kernel.transpose(1, 0, 2), *constants)
    return result[None, None, None]


def solution(mesh):
    return jax.shard_map(
        functools.partial(shards, sizes=dict(mesh.shape)),
        mesh=mesh,
        in_specs=(
            P("kx", "ky", "kz", None, None, "fft", None, None),
            P("kx", "ky", "kz", None, None, "fft", None, None),
            P("kx", "ky", "kz", None),
            P(None, "fft", None),
        ),
        out_specs=P("kx", "ky", "kz", None, None, "fft", None, None),
        check_vma=False,
    )
```

```python
import functools
import math

import jax
import jax.numpy as jnp
import ml_dtypes
import numpy as np
from jax import lax
from jax.experimental import pallas as pl
from jax.experimental.pallas import tpu as pltpu
from jax.sharding import PartitionSpec as P

MESH = pl.DeviceIdType.MESH
PAIRED = 2
GROUP = 4
TILE = GROUP * 2 * PAIRED


def dft_table(length, sign):
    index = np.arange(length)
    theta = (index[:, None] * index[None, :] % length) * (2.0 * math.pi / length)
    factor = 1.0 / math.sqrt(length)
    cosine = np.cos(theta) * factor
    sine = np.sin(theta) * (sign * factor)
    return np.stack([np.stack([cosine, -sine]), np.stack([sine, cosine])])


def tables(ring, planes, width_b, width_c):
    width_a = ring * planes
    slab = width_b // ring
    chunks = planes

    def c_table(sign):
        table = dft_table(width_c, sign)
        return table.transpose(1, 3, 0, 2).reshape(2 * width_c, 2 * width_c)

    forward = dft_table(width_b, -1.0).reshape(2, 2, ring, slab, width_b)
    b_forward = forward.transpose(2, 3, 0, 1, 4).reshape(2 * width_b, 2 * width_b)
    inverse = dft_table(width_b, 1.0).reshape(2, 2, width_b, ring, slab)
    b_inverse = inverse.transpose(0, 2, 3, 4, 1).reshape(2 * width_b, 2 * width_b)

    same, band = np.eye(GROUP), np.eye(PAIRED)
    size = 2 * PAIRED * GROUP * width_a
    forward = dft_table(width_a, -1.0).reshape(2, 2, width_a, ring, chunks)
    a_forward = np.einsum("oikyj,gh,nq->nogkjyhiq", forward, same, band).reshape(size, size)
    inverse = dft_table(width_a, 1.0).reshape(2, 2, ring, chunks, width_a)
    a_inverse = np.einsum("oiyjk,gh,nq->jygonqihk", inverse, same, band).reshape(size, size)
    return [
        t.astype(ml_dtypes.bfloat16)
        for t in (c_table(-1.0), c_table(1.0), b_forward, b_inverse, a_forward, a_inverse)
    ]


def dot(x, y):
    return jnp.dot(x, y, preferred_element_type=jnp.float32)


def kernel_body(
    dims,
    occ_hbm, tgt_hbm, w_ref, ker_hbm, c1_hbm, c2_hbm, b1_hbm, b2_hbm, a1_hbm, a2_hbm,
    out_hbm,
    occ, own, tgt, ker, c1, c2, b1, b2, a1, a2, w_own, w_got,
    mixed, send1, recv1, send2, recv2, acc, out,
    ready, load_sem, shift_send, shift_recv, w_send, w_recv,
    send1_sem, recv1_sem, send2_sem, recv2_sem, out_sem,
):
    sizes, bands, targets, planes, width_b, width_c = dims
    ring = sizes["fft"]
    chunks = planes
    slab = width_b // ring
    groups = slab // GROUP
    width_a = ring * planes
    me = lax.axis_index("fft")

    def moved(by):
        return {
            axis: lax.rem(lax.axis_index(axis) + (sizes[axis] + by), sizes[axis])
            for axis in ("kx", "ky", "kz")
        }

    ahead, behind = moved(1), moved(-1)
    order = [d for pair in zip(range(ring // 2, 0, -1), range(ring // 2, ring)) for d in pair]
    order = list(dict.fromkeys(order))

    def partner(d):
        return lax.rem(me + d, ring)

    place = lax.axis_index("kz")
    asks = place == sizes["kz"] // 2
    asked = place == sizes["kz"] // 2 - 1
    barrier = pltpu.get_barrier_semaphore()
    for d in order:
        pl.semaphore_signal(barrier, inc=1, device_id={"fft": partner(d)}, device_id_type=MESH)

    @pl.when(jnp.logical_not(asks))
    def _():
        pl.semaphore_signal(barrier, inc=1, device_id=behind, device_id_type=MESH)

    @pl.when(asked)
    def _():
        pl.semaphore_signal(barrier, inc=1, device_id=ahead, device_id_type=MESH)

    loads = [
        pltpu.make_async_copy(src, dst, load_sem.at[i])
        for i, (src, dst) in enumerate(
            (
                (tgt_hbm, tgt), (c1_hbm, c1), (b1_hbm, b1), (ker_hbm, ker),
                (a1_hbm, a1), (a2_hbm, a2), (b2_hbm, b2), (c2_hbm, c2), (occ_hbm, own),
            )
        )
    ]
    for load in loads[-1:] + loads[:-1]:
        load.start()
    for m in range(bands):
        w_own[m] = jnp.broadcast_to(
            w_ref[:, m : m + 1].astype(jnp.float32), w_own.shape[1:]
        ).astype(jnp.bfloat16)

    loads[-1].wait()
    pl.semaphore_wait(barrier, ring - 1 + jnp.where(asked, 0, 1) + jnp.where(asks, 1, 0))

    @pl.when(asks)
    def _():
        pl.semaphore_signal(ready, inc=1, device_id=behind, device_id_type=MESH)

    @pl.when(asked)
    def _():
        pl.semaphore_wait(ready, 1)

    def shift(m, j):
        part = (slice(None), m, j)
        return pltpu.make_async_remote_copy(
            src_ref=own.at[part],
            dst_ref=occ.at[part],
            send_sem=shift_send,
            recv_sem=shift_recv.at[m, j],
            device_id=ahead,
            device_id_type=MESH,
        )

    w_copy = pltpu.make_async_remote_copy(
        src_ref=w_own, dst_ref=w_got, send_sem=w_send, recv_sem=w_recv,
        device_id=ahead, device_id_type=MESH,
    )
    for m in range(bands):
        for j in range(chunks):
            shift(m, j).start()
    w_copy.start()

    def scatter(p, j, send, recv, send_sem, recv_sem):
        for d in order:
            to = partner(d)
            pltpu.make_async_remote_copy(
                src_ref=send.at[p, j, to],
                dst_ref=recv.at[p, j, me],
                send_sem=send_sem,
                recv_sem=recv_sem,
                device_id={"fft": to},
                device_id_type=MESH,
            ).start()
        pltpu.make_async_copy(send.at[p, j, me], recv.at[p, j, me], recv_sem).start()

    def ended(part, sem):
        pltpu.make_async_copy(part, part, sem).wait()

    for i in (0, 1, 2):
        loads[i].wait()

    def forward(step, _):
        m, j = step // chunks, lax.rem(step, chunks)
        shift(m, j).wait_recv()
        o_re, o_im = (occ[i, m, j].astype(jnp.float32) for i in range(2))
        pairs = []
        for n in range(targets):
            t_re, t_im = (tgt[i, n, j].astype(jnp.float32) for i in range(2))
            pairs.append(
                jnp.concatenate(
                    [
                        (o_re * t_re + o_im * t_im).astype(jnp.bfloat16),
                        (o_re * t_im - o_im * t_re).astype(jnp.bfloat16),
                    ],
                    axis=1,
                )
            )
        first = dot(jnp.concatenate(pairs, axis=0), c1[...]).astype(jnp.bfloat16)
        both = [first[n * width_b : (n + 1) * width_b] for n in range(targets)]
        lines = jnp.concatenate(
            [
                jnp.concatenate([x[:, :width_c] for x in both], axis=1),
                jnp.concatenate([x[:, width_c:] for x in both], axis=1),
            ],
            axis=0,
        )
        second = dot(b1[...], lines)
        for n in range(targets):
            mixed[pl.ds(n, 2 * width_b, stride=targets), :] = second[:, n * width_c : (n + 1) * width_c]
        send1[m, j] = mixed[...].astype(jnp.bfloat16).reshape(send1.shape[2:])
        scatter(m, j, send1, recv1, send1_sem, recv1_sem.at[m])
        return 0

    lax.fori_loop(0, bands * chunks, forward, 0)

    for i in (3, 4, 5, 6, 7):
        loads[i].wait()

    def middle(p, _):
        ended(recv1.at[p], recv1_sem.at[p])
        lines = jnp.concatenate(
            [
                recv1[p, :, :, g * TILE : (g + 1) * TILE, :].reshape(2 * PAIRED * GROUP * width_a, width_c)
                for g in range(groups)
            ],
            axis=1,
        )
        spectrum = dot(a1[...], lines)
        half = GROUP * width_a
        factor = [
            ker[g * GROUP : (g + 1) * GROUP].reshape(half, width_c).astype(jnp.float32)
            for g in range(groups)
        ]
        screened = jnp.concatenate(
            [
                jnp.concatenate(
                    [
                        spectrum[i * half : (i + 1) * half, g * width_c : (g + 1) * width_c] * factor[g]
                        for g in range(groups)
                    ],
                    axis=1,
                ).astype(jnp.bfloat16)
                for i in range(2 * PAIRED)
            ],
            axis=0,
        )
        back = dot(a2[...], screened).astype(jnp.bfloat16)
        for g in range(groups):
            send2[p, :, :, g * TILE : (g + 1) * TILE, :] = back[
                :, g * width_c : (g + 1) * width_c
            ].reshape(chunks, ring, TILE, width_c)
        for j in range(chunks):
            scatter(p, j, send2, recv2, send2_sem, recv2_sem.at[p, j])
        return 0

    lax.fori_loop(0, bands, middle, 0)

    w_copy.wait()
    ended(occ, shift_send)
    ended(send1.at[:, :, pl.ds(0, ring - 1)], send1_sem)

    def backward(m, j):
        ended(recv2.at[m, j], recv2_sem.at[m, j])
        mixed[...] = recv2[m, j].reshape(mixed.shape).astype(jnp.float32)
        lines = jnp.concatenate(
            [mixed[pl.ds(n, 2 * width_b, stride=targets), :] for n in range(targets)], axis=1
        ).astype(jnp.bfloat16)
        done = dot(b2[...], lines).astype(jnp.bfloat16)
        cuts = [done[:, n * width_c : (n + 1) * width_c] for n in range(targets)]
        lines = [jnp.concatenate([cut[:width_b], cut[width_b:]], axis=1) for cut in cuts]
        potential = dot(jnp.concatenate(lines, axis=0), c2[...])
        scale = w_got[m].astype(jnp.float32)[:1]
        o_re, o_im = (occ[i, m, j].astype(jnp.float32) * scale for i in range(2))
        for n in range(targets):
            part = potential[n * width_b : (n + 1) * width_b]
            v_re, v_im = part[:, :width_c], part[:, width_c:]
            sums = (o_re * v_re - o_im * v_im, o_re * v_im + o_im * v_re)
            for i in range(2):
                total = acc[i, n, j] + sums[i] if m > 0 else sums[i]
                if m == bands - 1:
                    out[i, n, j] = (-0.25 * total).astype(jnp.bfloat16)
                else:
                    acc[i, n, j] = total
        if m == bands - 1:
            store(j).start()
        return 0

    def store(j):
        part = (slice(None), slice(None), j)
        return pltpu.make_async_copy(out.at[part], out_hbm.at[part], out_sem)

    for m in range(bands):
        lax.fori_loop(0, chunks, lambda j, _, m=m: backward(m, j), 0)

    ended(send2.at[:, :, pl.ds(0, ring - 1)], send2_sem)
    ended(out, out_sem)


def shards(occupied, targets, weights, kernel, sizes):
    occ = occupied[0, 0, 0]
    tgt = targets[0, 0, 0]
    bands, tgts = occ.shape[1], tgt.shape[1]
    planes, width_b, width_c = occ.shape[2:]
    ring = sizes["fft"]
    width_a = ring * planes
    slab = width_b // ring
    chunks = planes
    groups = slab // GROUP
    constants = [jnp.asarray(t) for t in tables(ring, planes, width_b, width_c)]
    bf16, f32 = jnp.bfloat16, jnp.float32
    blocks = (bands, chunks, ring, slab * 2 * PAIRED, width_c)
    any_space = pl.BlockSpec(memory_space=pl.ANY)
    result = pl.pallas_call(
        functools.partial(kernel_body, (sizes, bands, tgts, planes, width_b, width_c)),
        out_shape=jax.ShapeDtypeStruct(tgt.shape, bf16),
        in_specs=[any_space, any_space, pl.BlockSpec(memory_space=pltpu.VMEM)] + [any_space] * 7,
        out_specs=any_space,
        scratch_shapes=[
            pltpu.VMEM(occ.shape, bf16),
            pltpu.VMEM(occ.shape, bf16),
            pltpu.VMEM(tgt.shape, bf16),
            pltpu.VMEM((slab, width_a, width_c), bf16),
            *[pltpu.VMEM(t.shape, bf16) for t in constants],
            pltpu.VMEM((bands, 16, width_c), bf16),
            pltpu.VMEM((bands, 16, width_c), bf16),
            pltpu.VMEM((2 * width_b * PAIRED, width_c), f32),
            *[pltpu.VMEM(blocks, bf16)] * 4,
            pltpu.VMEM((2, tgts, chunks, width_b, width_c), f32),
            pltpu.VMEM(tgt.shape, bf16),
            pltpu.SemaphoreType.REGULAR,
            pltpu.SemaphoreType.DMA((9,)),
            pltpu.SemaphoreType.DMA,
            pltpu.SemaphoreType.DMA((bands, chunks)),
            pltpu.SemaphoreType.DMA,
            pltpu.SemaphoreType.DMA,
            pltpu.SemaphoreType.DMA,
            pltpu.SemaphoreType.DMA((bands,)),
            pltpu.SemaphoreType.DMA,
            pltpu.SemaphoreType.DMA((bands, chunks)),
            pltpu.SemaphoreType.DMA,
        ],
        compiler_params=pltpu.CompilerParams(
            collective_id=0, has_side_effects=True, vmem_limit_bytes=56 << 20
        ),
    )(occ, tgt, weights.reshape(1, bands), kernel.transpose(1, 0, 2), *constants)
    return result[None, None, None]


def solution(mesh):
    return jax.shard_map(
        functools.partial(shards, sizes=dict(mesh.shape)),
        mesh=mesh,
        in_specs=(
            P("kx", "ky", "kz", None, None, "fft", None, None),
            P("kx", "ky", "kz", None, None, "fft", None, None),
            P("kx", "ky", "kz", None),
            P(None, "fft", None),
        ),
        out_specs=P("kx", "ky", "kz", None, None, "fft", None, None),
        check_vma=False,
    )
```

```python
import functools
import math

import jax
import jax.numpy as jnp
import ml_dtypes
import numpy as np
from jax import lax
from jax.experimental import pallas as pl
from jax.experimental.pallas import tpu as pltpu
from jax.sharding import PartitionSpec as P

MESH = pl.DeviceIdType.MESH
PAIRED = 2
GROUP = 4
TILE = GROUP * 2 * PAIRED


def dft_table(length, sign):
    index = np.arange(length)
    theta = (index[:, None] * index[None, :] % length) * (2.0 * math.pi / length)
    factor = 1.0 / math.sqrt(length)
    cosine = np.cos(theta) * factor
    sine = np.sin(theta) * (sign * factor)
    return np.stack([np.stack([cosine, -sine]), np.stack([sine, cosine])])


def tables(ring, planes, width_b, width_c):
    width_a = ring * planes
    slab = width_b // ring
    chunks = planes

    def c_table(sign):
        table = dft_table(width_c, sign)
        return table.transpose(1, 3, 0, 2).reshape(2 * width_c, 2 * width_c)

    forward = dft_table(width_b, -1.0).reshape(2, 2, ring, slab, width_b)
    b_forward = forward.transpose(2, 3, 0, 1, 4).reshape(2 * width_b, 2 * width_b)
    inverse = dft_table(width_b, 1.0).reshape(2, 2, width_b, ring, slab)
    b_inverse = inverse.transpose(0, 2, 3, 4, 1).reshape(2 * width_b, 2 * width_b)

    same, band = np.eye(GROUP), np.eye(PAIRED)
    size = 2 * PAIRED * GROUP * width_a
    forward = dft_table(width_a, -1.0).reshape(2, 2, width_a, ring, chunks)
    a_forward = np.einsum("oikyj,gh,nq->nogkjyhiq", forward, same, band).reshape(size, size)
    inverse = dft_table(width_a, 1.0).reshape(2, 2, ring, chunks, width_a)
    a_inverse = np.einsum("oiyjk,gh,nq->jygonqihk", inverse, same, band).reshape(size, size)
    return [
        t.astype(ml_dtypes.bfloat16)
        for t in (c_table(-1.0), c_table(1.0), b_forward, b_inverse, a_forward, a_inverse)
    ]


def dot(x, y):
    return jnp.dot(x, y, preferred_element_type=jnp.float32)


def kernel_body(
    dims,
    occ_hbm, tgt_hbm, w_ref, ker_hbm, c1_hbm, c2_hbm, b1_hbm, b2_hbm, a1_hbm, a2_hbm,
    out_hbm,
    occ, own, tgt, ker, c1, c2, b1, b2, a1, a2, w_own, w_got,
    mixed, send1, recv1, send2, recv2, acc, out,
    ready, load_sem, shift_send, shift_recv, w_send, w_recv,
    send1_sem, recv1_sem, send2_sem, recv2_sem, out_sem,
):
    sizes, bands, targets, planes, width_b, width_c = dims
    ring = sizes["fft"]
    chunks = planes
    slab = width_b // ring
    groups = slab // GROUP
    width_a = ring * planes
    me = lax.axis_index("fft")

    def moved(by):
        return {
            axis: lax.rem(lax.axis_index(axis) + (sizes[axis] + by), sizes[axis])
            for axis in ("kx", "ky", "kz")
        }

    ahead, behind = moved(1), moved(-1)
    order = [d for pair in zip(range(ring // 2, 0, -1), range(ring // 2, ring)) for d in pair]
    order = list(dict.fromkeys(order))

    def partner(d):
        return lax.rem(me + d, ring)

    place = lax.axis_index("kz")
    asks = place == sizes["kz"] // 2
    asked = place == sizes["kz"] // 2 - 1
    barrier = pltpu.get_barrier_semaphore()
    for d in order:
        pl.semaphore_signal(barrier, inc=1, device_id={"fft": partner(d)}, device_id_type=MESH)

    @pl.when(jnp.logical_not(asks))
    def _():
        pl.semaphore_signal(barrier, inc=1, device_id=behind, device_id_type=MESH)

    @pl.when(asked)
    def _():
        pl.semaphore_signal(barrier, inc=1, device_id=ahead, device_id_type=MESH)

    loads = [
        pltpu.make_async_copy(src, dst, load_sem.at[i])
        for i, (src, dst) in enumerate(
            (
                (tgt_hbm, tgt), (c1_hbm, c1), (b1_hbm, b1), (ker_hbm, ker),
                (a1_hbm, a1), (a2_hbm, a2), (b2_hbm, b2), (c2_hbm, c2), (occ_hbm, own),
            )
        )
    ]
    for load in loads[-1:] + loads[:-1]:
        load.start()
    for m in range(bands):
        w_own[m] = jnp.broadcast_to(
            w_ref[:, m : m + 1].astype(jnp.float32), w_own.shape[1:]
        ).astype(jnp.bfloat16)

    loads[-1].wait()
    pl.semaphore_wait(barrier, ring - 1 + jnp.where(asked, 0, 1) + jnp.where(asks, 1, 0))

    @pl.when(asks)
    def _():
        pl.semaphore_signal(ready, inc=1, device_id=behind, device_id_type=MESH)

    def shift(m, j):
        part = (slice(None), m, j)
        return pltpu.make_async_remote_copy(
            src_ref=own.at[part],
            dst_ref=occ.at[part],
            send_sem=shift_send,
            recv_sem=shift_recv.at[m, j],
            device_id=ahead,
            device_id_type=MESH,
        )

    w_copy = pltpu.make_async_remote_copy(
        src_ref=w_own, dst_ref=w_got, send_sem=w_send, recv_sem=w_recv,
        device_id=ahead, device_id_type=MESH,
    )
    def send_ahead():
        def one(step, _):
            shift(step // chunks, lax.rem(step, chunks)).start()
            return 0

        lax.fori_loop(0, bands * chunks, one, 0)
        w_copy.start()

    @pl.when(jnp.logical_not(asked))
    def _():
        send_ahead()


    def scatter(p, j, send, recv, send_sem, recv_sem):
        for d in order:
            to = partner(d)
            pltpu.make_async_remote_copy(
                src_ref=send.at[p, j, to],
                dst_ref=recv.at[p, j, me],
                send_sem=send_sem,
                recv_sem=recv_sem,
                device_id={"fft": to},
                device_id_type=MESH,
            ).start()
        pltpu.make_async_copy(send.at[p, j, me], recv.at[p, j, me], recv_sem).start()

    def ended(part, sem):
        pltpu.make_async_copy(part, part, sem).wait()

    for i in (0, 1, 2):
        loads[i].wait()

    def forward(step, _):
        m, j = step // chunks, lax.rem(step, chunks)

        @pl.when(jnp.logical_and(asked, step == 2))
        def _():
            pl.semaphore_wait(ready, 1)
            send_ahead()

        shift(m, j).wait_recv()
        o_re, o_im = (occ[i, m, j].astype(jnp.float32) for i in range(2))
        pairs = []
        for n in range(targets):
            t_re, t_im = (tgt[i, n, j].astype(jnp.float32) for i in range(2))
            pairs.append(
                jnp.concatenate(
                    [
                        (o_re * t_re + o_im * t_im).astype(jnp.bfloat16),
                        (o_re * t_im - o_im * t_re).astype(jnp.bfloat16),
                    ],
                    axis=1,
                )
            )
        first = dot(jnp.concatenate(pairs, axis=0), c1[...]).astype(jnp.bfloat16)
        both = [first[n * width_b : (n + 1) * width_b] for n in range(targets)]
        lines = jnp.concatenate(
            [
                jnp.concatenate([x[:, :width_c] for x in both], axis=1),
                jnp.concatenate([x[:, width_c:] for x in both], axis=1),
            ],
            axis=0,
        )
        second = dot(b1[...], lines)
        for n in range(targets):
            mixed[pl.ds(n, 2 * width_b, stride=targets), :] = second[:, n * width_c : (n + 1) * width_c]
        send1[m, j] = mixed[...].astype(jnp.bfloat16).reshape(send1.shape[2:])
        scatter(m, j, send1, recv1, send1_sem, recv1_sem.at[m])
        return 0

    lax.fori_loop(0, bands * chunks, forward, 0)

    for i in (3, 4, 5, 6, 7):
        loads[i].wait()

    def middle(p, _):
        ended(recv1.at[p], recv1_sem.at[p])
        lines = jnp.concatenate(
            [
                recv1[p, :, :, g * TILE : (g + 1) * TILE, :].reshape(2 * PAIRED * GROUP * width_a, width_c)
                for g in range(groups)
            ],
            axis=1,
        )
        spectrum = dot(a1[...], lines)
        half = GROUP * width_a
        factor = [
            ker[g * GROUP : (g + 1) * GROUP].reshape(half, width_c).astype(jnp.float32)
            for g in range(groups)
        ]
        screened = jnp.concatenate(
            [
                jnp.concatenate(
                    [
                        spectrum[i * half : (i + 1) * half, g * width_c : (g + 1) * width_c] * factor[g]
                        for g in range(groups)
                    ],
                    axis=1,
                ).astype(jnp.bfloat16)
                for i in range(2 * PAIRED)
            ],
            axis=0,
        )
        back = dot(a2[...], screened).astype(jnp.bfloat16)
        for g in range(groups):
            send2[p, :, :, g * TILE : (g + 1) * TILE, :] = back[
                :, g * width_c : (g + 1) * width_c
            ].reshape(chunks, ring, TILE, width_c)
        for j in range(chunks):
            scatter(p, j, send2, recv2, send2_sem, recv2_sem.at[p, j])
        return 0

    lax.fori_loop(0, bands, middle, 0)

    w_copy.wait()
    ended(occ, shift_send)
    ended(send1.at[:, :, pl.ds(0, ring - 1)], send1_sem)

    def backward(m, j):
        ended(recv2.at[m, j], recv2_sem.at[m, j])
        mixed[...] = recv2[m, j].reshape(mixed.shape).astype(jnp.float32)
        lines = jnp.concatenate(
            [mixed[pl.ds(n, 2 * width_b, stride=targets), :] for n in range(targets)], axis=1
        ).astype(jnp.bfloat16)
        done = dot(b2[...], lines).astype(jnp.bfloat16)
        cuts = [done[:, n * width_c : (n + 1) * width_c] for n in range(targets)]
        lines = [jnp.concatenate([cut[:width_b], cut[width_b:]], axis=1) for cut in cuts]
        potential = dot(jnp.concatenate(lines, axis=0), c2[...])
        scale = w_got[m].astype(jnp.float32)[:1]
        o_re, o_im = (occ[i, m, j].astype(jnp.float32) * scale for i in range(2))
        for n in range(targets):
            part = potential[n * width_b : (n + 1) * width_b]
            v_re, v_im = part[:, :width_c], part[:, width_c:]
            sums = (o_re * v_re - o_im * v_im, o_re * v_im + o_im * v_re)
            for i in range(2):
                total = acc[i, n, j] + sums[i] if m > 0 else sums[i]
                if m == bands - 1:
                    out[i, n, j] = (-0.25 * total).astype(jnp.bfloat16)
                else:
                    acc[i, n, j] = total
        if m == bands - 1:
            store(j).start()
        return 0

    def store(j):
        part = (slice(None), slice(None), j)
        return pltpu.make_async_copy(out.at[part], out_hbm.at[part], out_sem)

    for m in range(bands):
        lax.fori_loop(0, chunks, lambda j, _, m=m: backward(m, j), 0)

    ended(send2.at[:, :, pl.ds(0, ring - 1)], send2_sem)
    ended(out, out_sem)


def shards(occupied, targets, weights, kernel, sizes):
    occ = occupied[0, 0, 0]
    tgt = targets[0, 0, 0]
    bands, tgts = occ.shape[1], tgt.shape[1]
    planes, width_b, width_c = occ.shape[2:]
    ring = sizes["fft"]
    width_a = ring * planes
    slab = width_b // ring
    chunks = planes
    groups = slab // GROUP
    constants = [jnp.asarray(t) for t in tables(ring, planes, width_b, width_c)]
    bf16, f32 = jnp.bfloat16, jnp.float32
    blocks = (bands, chunks, ring, slab * 2 * PAIRED, width_c)
    any_space = pl.BlockSpec(memory_space=pl.ANY)
    result = pl.pallas_call(
        functools.partial(kernel_body, (sizes, bands, tgts, planes, width_b, width_c)),
        out_shape=jax.ShapeDtypeStruct(tgt.shape, bf16),
        in_specs=[any_space, any_space, pl.BlockSpec(memory_space=pltpu.VMEM)] + [any_space] * 7,
        out_specs=any_space,
        scratch_shapes=[
            pltpu.VMEM(occ.shape, bf16),
            pltpu.VMEM(occ.shape, bf16),
            pltpu.VMEM(tgt.shape, bf16),
            pltpu.VMEM((slab, width_a, width_c), bf16),
            *[pltpu.VMEM(t.shape, bf16) for t in constants],
            pltpu.VMEM((bands, 16, width_c), bf16),
            pltpu.VMEM((bands, 16, width_c), bf16),
            pltpu.VMEM((2 * width_b * PAIRED, width_c), f32),
            *[pltpu.VMEM(blocks, bf16)] * 4,
            pltpu.VMEM((2, tgts, chunks, width_b, width_c), f32),
            pltpu.VMEM(tgt.shape, bf16),
            pltpu.SemaphoreType.REGULAR,
            pltpu.SemaphoreType.DMA((9,)),
            pltpu.SemaphoreType.DMA,
            pltpu.SemaphoreType.DMA((bands, chunks)),
            pltpu.SemaphoreType.DMA,
            pltpu.SemaphoreType.DMA,
            pltpu.SemaphoreType.DMA,
            pltpu.SemaphoreType.DMA((bands,)),
            pltpu.SemaphoreType.DMA,
            pltpu.SemaphoreType.DMA((bands, chunks)),
            pltpu.SemaphoreType.DMA,
        ],
        compiler_params=pltpu.CompilerParams(
            collective_id=0, has_side_effects=True, vmem_limit_bytes=56 << 20
        ),
    )(occ, tgt, weights.reshape(1, bands), kernel.transpose(1, 0, 2), *constants)
    return result[None, None, None]


def solution(mesh):
    return jax.shard_map(
        functools.partial(shards, sizes=dict(mesh.shape)),
        mesh=mesh,
        in_specs=(
            P("kx", "ky", "kz", None, None, "fft", None, None),
            P("kx", "ky", "kz", None, None, "fft", None, None),
            P("kx", "ky", "kz", None),
            P(None, "fft", None),
        ),
        out_specs=P("kx", "ky", "kz", None, None, "fft", None, None),
        check_vma=False,
    )
```
